32 devices in a mesh: ctx: 16 (over z, y, core), dp: 2 (over x).
Axes of the slice: x: 2, y: 2, z: 4, core: 2. Of those that a mesh axis runs over, the one named last changes fastest.
Arguments:
- query_rows: bfloat16 [2, 2048, 1024], P('dp', 'ctx'), may hold values from -6 to 6
- key_rows: bfloat16 [2, 2048, 1024], P('dp', 'ctx'), may hold values from -6 to 6
- value_rows: bfloat16 [2, 2048, 1024], P('dp', 'ctx'), may hold values from -6 to 6
- block_lists: int32 [2, 16, 4], P('dp'), may hold values from 0 to 15, as said below
- block_lengths: int32 [2, 16], P('dp'), may hold values from 2 to 128, as said below
- out_weight: bfloat16 [1024, 2048], replicated, may hold values from -0.125 to 0.125
- expert_input: bfloat16 [2, 2048, 2048], P('dp', 'ctx'), may hold values from -6 to 6
- layer_grad: bfloat16 [2, 2048, 2048], P('dp', 'ctx'), may hold values from -1.5 to 1.5
- route_experts: int32 [2, 2048, 6], P('dp', 'ctx'), may hold values from 0 to 15, all different within a row; in each aligned block of 128 rows (0 to 127, 128 to 255, ..., all dimensions but the last counted through in order) at most 64 rows name the same one
- route_weight: float32 [2, 2048, 6], P('dp', 'ctx'), may hold values from 0.02 to 0.4
- gate_weight: bfloat16 [16, 2048, 704], P('ctx'), may hold values from -0.125 to 0.125
- up_weight: bfloat16 [16, 2048, 704], P('ctx'), may hold values from -0.125 to 0.125
- down_weight: bfloat16 [16, 2048, 704], P('ctx'), may hold values from -0.21875 to 0.21875
Outputs:
- query_grad: bfloat16 [2, 2048, 1024], P('dp', 'ctx')
- key_grad: bfloat16 [2, 2048, 1024], P('dp', 'ctx')
- value_grad: bfloat16 [2, 2048, 1024], P('dp', 'ctx')
- gate_grad: float32 [16, 2048, 704], P('ctx', 'dp')
- up_grad: float32 [16, 2048, 704], P('ctx', 'dp')
- down_grad: float32 [16, 2048, 704], P('ctx', 'dp')
The draws below stay inside these ranges and needn't reach their ends.
Inputs may be any that keep to these rules, and one draw needn't show every extreme that they name: `block_lists`: entry 0 of row i of a sequence's lists is i; every entry of row i lies in 0 to i. `block_lengths`: every sequence has a block of full length 128. `route_experts`: each token names 6 different experts. Among the 128 tokens of one device, no expert is named by more than 64 tokens.
All inputs are finite; a program needn't handle non-finite values.
Results may differ from the reference program's by a relative error of at most 0.012.
The reference program's roundings to bfloat16 on the way count: a program that leaves them out, or rounds other values in their place, can miss the bound.
Values may be sent and summed in bfloat16 or wider, within the bound.
A program may use at most 192 MiB of HBM per device.

```python
import math
from functools import partial
import jax
import jax.numpy as jnp
import numpy as np
from jax import lax

D = 2048
HEADS = 8
HD = 128
FFE = 704
TOPK = 6
BLK = 128
NSEL = 4
S_DEV = 128
SEQS = 2
LEN = 2048
NBLK = 16
EXPERTS = 16
CAP = 64
N_CTX = 16


def query_key_pair(key):
    base_key = jax.random.fold_in(key, 11)
    array_shape = (SEQS, LEN, HEADS * HD)
    queries = jax.random.truncated_normal(jax.random.fold_in(base_key, 1), -6.0, 6.0, array_shape, jnp.float32)
    keys_drawn = jax.random.truncated_normal(jax.random.fold_in(base_key, 2), -6.0, 6.0, array_shape, jnp.float32)
    return (queries, keys_drawn)


def draw_query_rows(key, part):
    return query_key_pair(key)[0].astype(jnp.bfloat16)


def draw_key_rows(key, part):
    return query_key_pair(key)[1].astype(jnp.bfloat16)


def draw_block_lists(key, part):
    block_rows = jnp.arange(NBLK, dtype=jnp.int32)
    upper_bound = jnp.broadcast_to((block_rows + 1)[None, :, None], (SEQS, NBLK, NSEL - 1))
    extra_blocks = jax.random.randint(jax.random.fold_in(key, 21), (SEQS, NBLK, NSEL - 1), 0, upper_bound, dtype=jnp.int32)
    diagonal = jnp.broadcast_to(block_rows[None, :, None], (SEQS, NBLK, 1))
    return jnp.concatenate([diagonal, extra_blocks], axis=2).astype(jnp.int32)


def draw_block_lengths(key, part):
    lengths = jax.random.randint(jax.random.fold_in(key, 31), (SEQS, NBLK), 2, BLK + 1, dtype=jnp.int32)
    full_block = jax.random.randint(jax.random.fold_in(key, 32), (SEQS, 1), 0, NBLK, dtype=jnp.int32)
    is_full = jnp.arange(NBLK, dtype=jnp.int32)[None, :] == full_block
    return jnp.where(is_full, BLK, lengths).astype(jnp.int32)


def block_levels(key, shape, cuts, least, largest):
    def one(position, shards_of):
        draws = jax.random.uniform(jax.random.fold_in(jax.random.fold_in(key, 6), position), (shards_of,), jnp.float32, least / len(cuts), largest / len(cuts))
        return jnp.repeat(jnp.exp(draws), shape[position] // shards_of).reshape((-1,) + (1,) * (len(shape) - position - 1))

    gain = one(*cuts[0])
    for cut in cuts[1:]:
        gain = gain * one(*cut)
    return gain


def deal_out(stream_key, own, number, rows, amount, top, limit, skew):
    order = jax.random.permutation(stream_key, amount)
    packed, ordinary = portions_of(amount, rows * top, limit, skew, True), portions_of(amount, rows * top, limit, skew, False)
    places = jnp.arange(amount)

    def named(sizes, rotation):
        used = int((sizes > 0).sum())
        fixed = max(1, used // 4)
        passed = fixed + (places - fixed + rotation * (used - fixed)) % max(1, amount - fixed)
        return jnp.zeros((amount,), jnp.int32).at[order[jnp.where(places < fixed, places, passed)]].set(jnp.asarray(sizes, jnp.int32))

    sizes = jnp.where(number % 4 == 0, named(packed, number // 4), named(ordinary, number - number // 4 - 1))
    mixed = jax.random.permutation(jax.random.fold_in(own, 3), amount)
    donor, sink = mixed[0:amount // 2 * 2:2], mixed[1:amount // 2 * 2:2]
    margin = jnp.minimum(sizes[donor] - 1, limit - sizes[sink]) // 2
    margin = jnp.where((donor == order[0]) | (sink == order[0]) | (sizes[sink] == 0), 0, jnp.maximum(margin, 0))
    passed = jax.random.randint(jax.random.fold_in(own, 4), (amount // 2,), 0, 1 << 20) % (margin + 1)
    sizes = sizes.at[donor].add(-passed).at[sink].add(passed)
    items = jnp.searchsorted(jnp.cumsum(sizes), jnp.arange(rows * top), side="right").astype(jnp.int32)
    grid = items.reshape(top, rows).T
    grid = grid[jax.random.permutation(jax.random.fold_in(own, 1), rows)]
    rotation = jax.random.randint(jax.random.fold_in(own, 2), (rows, 1), 0, top)
    return jnp.take_along_axis(grid, (jnp.arange(top)[None, :] + rotation) % top, axis=1)


def portions_of(number_of, total, most, lean, full):
    portions = [(1 << 20) // math.isqrt(standing ** lean) + 1 for standing in range(1, number_of + 1)]
    largest = most if full else min(most, max(-(-total // number_of), total * portions[0] // sum(portions)))
    least = 1 if total - largest >= number_of - 1 else 0
    counts, rest = [largest] + [least] * (number_of - 1), total - largest - least * (number_of - 1)
    while rest > 0:
        free = [i for i in range(1, number_of) if counts[i] < largest] or [i for i in range(1, number_of) if counts[i] < most]
        pool, left = sum([portions[i] for i in free]), rest
        for i in free:
            extra = min(most - counts[i], max(1, left * portions[i] // pool), rest)
            counts[i] = counts[i] + extra
            rest = rest - extra
    return np.array(counts)


def scatter_about(own_key, shape, scale, bound, shards=(), kind=jnp.bfloat16):
    level = block_levels(own_key, shape, shards, -0.22, 0.18) if shards else 1.0
    entries = jax.random.normal(own_key, shape, jnp.float32) * scale * level
    return jnp.minimum(jnp.maximum(entries, -bound), bound).astype(kind)


def setup_inputs(seed: int = 0) -> dict:
    arg_keys = jax.random.split(jax.random.key(seed), 14)
    query_rows = draw_query_rows(jax.random.fold_in(arg_keys[13], 71), 0)
    key_rows = draw_key_rows(jax.random.fold_in(arg_keys[13], 71), 0)
    value_rows = scatter_about(arg_keys[2], (SEQS, LEN, HEADS * HD), 1.0, 6.0, ((0, 2), (1, 16)))
    block_lists = draw_block_lists(jax.random.fold_in(arg_keys[13], 71), 0)
    block_lengths = draw_block_lengths(jax.random.fold_in(arg_keys[13], 71), 0)
    out_weight = scatter_about(arg_keys[5], (HEADS * HD, D), D ** -0.5, 0.125)
    expert_input = scatter_about(arg_keys[6], (SEQS, LEN, D), 1.0, 6.0, ((0, 2), (1, 16)))
    layer_grad = scatter_about(arg_keys[7], (SEQS, LEN, D), 0.25, 1.5, ((0, 2), (1, 16)))
    route_experts_keys = jax.random.split(jax.random.fold_in(arg_keys[8], 1), SEQS * LEN // S_DEV)
    route_experts_turns = jax.random.permutation(jax.random.fold_in(arg_keys[8], 3), SEQS * LEN // S_DEV)
    route_experts = jax.vmap(lambda own, number: deal_out(jax.random.fold_in(arg_keys[8], 2), own, number, S_DEV, EXPERTS, TOPK, CAP, 2))(route_experts_keys, route_experts_turns).reshape((SEQS, LEN, TOPK))
    route_weight = jnp.clip(jnp.exp(math.log(0.4) - 2.9957323 * jax.random.uniform(arg_keys[9], (SEQS, LEN, TOPK), jnp.float32) ** block_levels(arg_keys[9], (SEQS, LEN, TOPK), ((0, 2), (1, 16)), -0.2, 0.2)), 0.02, 0.4)
    gate_weight = scatter_about(arg_keys[10], (EXPERTS, D, FFE), D ** -0.5, 0.125, ((0, 16),))
    up_weight = scatter_about(arg_keys[11], (EXPERTS, D, FFE), D ** -0.5, 0.125, ((0, 16),))
    down_weight = scatter_about(arg_keys[12], (EXPERTS, D, FFE), FFE ** -0.5, 0.21875, ((0, 16),))
    return {"query_rows": query_rows, "key_rows": key_rows, "value_rows": value_rows, "block_lists": block_lists, "block_lengths": block_lengths, "out_weight": out_weight, "expert_input": expert_input, "layer_grad": layer_grad, "route_experts": route_experts, "route_weight": route_weight, "gate_weight": gate_weight, "up_weight": up_weight, "down_weight": down_weight}


def build_table(lists_row):
    numbers = jnp.arange(NBLK, dtype=jnp.int32)
    return jnp.any(lists_row[:, :, None] == numbers[None, None, :], axis=1)

def block_mask(table_mask, lengths_row, query_start, query_count, key_start, key_count):
    first_query = jnp.asarray(query_start, jnp.int32) // BLK
    first_key = jnp.asarray(key_start, jnp.int32) // BLK
    tile_part = lax.dynamic_slice(table_mask, (first_query, first_key), (query_count // BLK, key_count // BLK))
    spread = jnp.broadcast_to(tile_part[:, None, :, None], (query_count // BLK, BLK, key_count // BLK, BLK)).reshape(query_count, key_count)
    lengths_part = lax.dynamic_slice_in_dim(lengths_row, first_key, key_count // BLK, 0)
    offsets = jnp.arange(BLK, dtype=jnp.int32)
    present = (offsets[None, :] < lengths_part[:, None]).reshape(key_count)
    query_pos = jnp.asarray(query_start, jnp.int32) + jnp.arange(query_count, dtype=jnp.int32)
    key_pos = jnp.asarray(key_start, jnp.int32) + jnp.arange(key_count, dtype=jnp.int32)
    return spread & present[None, :] & (query_pos[:, None] >= key_pos[None, :])

def round_low(values):
    return lax.optimization_barrier(values.astype(jnp.bfloat16)).astype(jnp.float32)

def attention_sequence(queries, keys_all, values_all, lists_row, lengths_row, grads_in, out_weight):
    inv_root = 1.0 / math.sqrt(HD)
    out_grad = jnp.dot(grads_in, out_weight.T, preferred_element_type=jnp.float32).astype(jnp.bfloat16)
    table_mask = build_table(lists_row)
    query_heads = queries.astype(jnp.float32).reshape(LEN, HEADS, HD)
    key_heads = keys_all.astype(jnp.float32).reshape(LEN, HEADS, HD)
    value_heads = values_all.astype(jnp.float32).reshape(LEN, HEADS, HD)
    grad_heads = out_grad.astype(jnp.float32).reshape(LEN, HEADS, HD)
    row_block = min(LEN, 512)
    row_steps = LEN // row_block

    def row_step(running, step_index):
        row_start = step_index * row_block
        query_part = lax.dynamic_slice_in_dim(query_heads, row_start, row_block, 0)
        grad_part = lax.dynamic_slice_in_dim(grad_heads, row_start, row_block, 0)
        allowed = block_mask(table_mask, lengths_row, row_start, row_block, 0, LEN)
        raw_scores = jnp.einsum('qhd,khd->hqk', query_part, key_heads) * inv_root
        scores = jnp.where(allowed[None], raw_scores, -jnp.inf)
        row_max = lax.optimization_barrier(jnp.max(scores, axis=2, keepdims=True))
        log_total = row_max + jnp.log(lax.optimization_barrier(jnp.sum(jnp.exp(scores - row_max), axis=2, keepdims=True)))
        prob_full = jnp.exp(scores - log_total)
        prob_low = round_low(prob_full)
        head_output = jnp.einsum('hqk,khd->hqd', prob_low, value_heads)
        row_delta = lax.optimization_barrier(jnp.sum(jnp.swapaxes(head_output, 0, 1) * grad_part, axis=2))
        prob_grad = jnp.einsum('qhd,khd->hqk', grad_part, value_heads)
        dscore = round_low(prob_full * (prob_grad - row_delta.T[:, :, None]))
        query_block = (jnp.einsum('hqk,khd->qhd', dscore, key_heads) * inv_root).astype(jnp.bfloat16)
        key_acc = running[0] + jnp.einsum('hqk,qhd->khd', dscore, query_part) * inv_root
        value_acc = running[1] + jnp.einsum('hqk,qhd->khd', prob_low, grad_part)
        return ((key_acc, value_acc), query_block)
    zero_rows = jnp.zeros((LEN, HEADS, HD), jnp.float32)
    (key_acc, value_acc), query_blocks = lax.scan(row_step, (zero_rows, zero_rows), jnp.arange(row_steps, dtype=jnp.int32))
    query_grad = query_blocks.reshape(LEN, HEADS * HD)
    key_grad = key_acc.reshape(LEN, HEADS * HD).astype(jnp.bfloat16)
    value_grad = value_acc.reshape(LEN, HEADS * HD).astype(jnp.bfloat16)
    return (query_grad, key_grad, value_grad)

def route_coefficients(chosen, rweights, expert_list):
    matches = chosen[:, :, None] == expert_list[None, None, :]
    return lax.optimization_barrier(jnp.sum(jnp.where(matches, rweights[:, :, None], 0.0), axis=1))

def slot_rows(tokens, grad_rows, coef_rows, capacity):
    present = coef_rows > 0.0
    rank_rows = jnp.cumsum(present.astype(jnp.int32), axis=0) - 1
    slot_ids = jnp.arange(capacity, dtype=jnp.int32)
    chosen_slot = present.T[:, None, :] & (rank_rows.T[:, None, :] == slot_ids[None, :, None])
    onehot = chosen_slot.astype(jnp.float32)
    picked = jnp.einsum('ecs,sd->ecd', onehot, tokens.astype(jnp.float32)).astype(jnp.bfloat16)
    picked_grad = jnp.einsum('ecs,sd->ecd', onehot, grad_rows.astype(jnp.float32))
    slot_coef = lax.optimization_barrier(jnp.sum(jnp.where(chosen_slot, coef_rows.T[:, None, :], 0.0), axis=2))
    scaled = (slot_coef[:, :, None] * picked_grad).astype(jnp.bfloat16)
    return (picked, scaled)

def reference(query_rows, key_rows, value_rows, block_lists, block_lengths, out_weight, expert_input, layer_grad, route_experts, route_weight, gate_weight, up_weight, down_weight):

    def one_sequence(seq_index):
        return attention_sequence(query_rows[seq_index], key_rows[seq_index], value_rows[seq_index], block_lists[seq_index], block_lengths[seq_index], layer_grad[seq_index], out_weight)
    query_grad, key_grad, value_grad = lax.map(one_sequence, jnp.arange(SEQS, dtype=jnp.int32))
    block_count = SEQS * N_CTX
    token_blocks = expert_input.reshape(block_count, S_DEV, D)
    grad_blocks = layer_grad.reshape(block_count, S_DEV, D)
    chosen_blocks = route_experts.reshape(block_count, S_DEV, TOPK)
    weight_blocks = route_weight.reshape(block_count, S_DEV, TOPK)

    def one_expert(expert):
        expert_list = jnp.reshape(expert, (1,)).astype(jnp.int32)
        coef_all = jax.vmap(route_coefficients, in_axes=(0, 0, None))(chosen_blocks, weight_blocks, expert_list)
        picked, scaled = jax.vmap(partial(slot_rows, capacity=CAP))(token_blocks, grad_blocks, coef_all)
        rows_in = picked.reshape(SEQS, N_CTX * CAP, D).astype(jnp.float32)
        grads_in = scaled.reshape(SEQS, N_CTX * CAP, D).astype(jnp.float32)
        gate_pre = jnp.einsum('srd,df->srf', rows_in, gate_weight[expert].astype(jnp.float32))
        up_pre = jnp.einsum('srd,df->srf', rows_in, up_weight[expert].astype(jnp.float32))
        gate_sig = jax.nn.sigmoid(gate_pre)
        gate_act = gate_pre * gate_sig
        hidden = round_low(gate_act * up_pre)
        down_part = jnp.einsum('srd,srf->sdf', grads_in, hidden).astype(jnp.bfloat16)
        hidden_grad = jnp.einsum('srd,df->srf', grads_in, down_weight[expert].astype(jnp.float32))
        gate_delta = round_low(hidden_grad * up_pre * gate_sig * (1.0 + gate_pre * (1.0 - gate_sig)))
        up_delta = round_low(hidden_grad * gate_act)
        gate_part = jnp.einsum('srd,srf->sdf', rows_in, gate_delta).astype(jnp.bfloat16)
        up_part = jnp.einsum('srd,srf->sdf', rows_in, up_delta).astype(jnp.bfloat16)
        return (lax.optimization_barrier(jnp.sum(gate_part.astype(jnp.float32), axis=0)), lax.optimization_barrier(jnp.sum(up_part.astype(jnp.float32), axis=0)), lax.optimization_barrier(jnp.sum(down_part.astype(jnp.float32), axis=0)))
    gate_grad, up_grad, down_grad = lax.map(one_expert, jnp.arange(EXPERTS, dtype=jnp.int32))
    return (query_grad, key_grad, value_grad, gate_grad, up_grad, down_grad)
```

```python
import functools
import math

import jax
import jax.numpy as jnp
from jax import lax
from jax.experimental import pallas as pl
from jax.experimental.pallas import tpu as pltpu
from jax.sharding import PartitionSpec as P

HEADS = 8
HD = 128
TOPK = 6
BLK = 128
INV_ROOT = 1.0 / math.sqrt(HD)
MESH = pl.DeviceIdType.MESH


def ring_gather_kernel(n, x_ref, g_ref, xo_ref, go_ref, ring_send, ring_recv, sib_send, sib_recv, own_sem):
    chips = n // 2
    half_chips = chips // 2
    rows = x_ref.shape[0]
    me = lax.axis_index("ctx")
    core = me % 2
    chip = me // 2
    z, y = chip // 2, chip % 2
    pos = z + y * (chips - 1 - 2 * z)

    def device_at(p):
        p = (p + 2 * chips) % chips
        hi = p // half_chips
        return 2 * (2 * p + hi * (2 * chips - 1 - 4 * p)) + core

    sibling = me + 1 - 2 * core
    nexts = (device_at(pos + 1), device_at(pos - 1))
    ins, outs = (x_ref, g_ref), (xo_ref, go_ref)

    def piece(owner, direction, hop):
        if hop < half_chips:
            return pl.ds(pl.multiple_of(owner * rows, rows), rows)
        part = rows // 2
        return pl.ds(pl.multiple_of(owner * rows + direction * part, part), part)

    def ring_copy(src, owner, a, direction, hop):
        return pltpu.make_async_remote_copy(
            src_ref=src,
            dst_ref=outs[a].at[piece(owner, direction, hop)],
            send_sem=ring_send.at[direction, hop - 1, a],
            recv_sem=ring_recv.at[direction, hop - 1, a],
            device_id={"ctx": nexts[direction]},
            device_id_type=MESH,
        )

    def sib_copy(src, dst, a, slot):
        return pltpu.make_async_remote_copy(
            src_ref=src,
            dst_ref=dst,
            send_sem=sib_send.at[slot, a],
            recv_sem=sib_recv.at[slot, a],
            device_id={"ctx": sibling},
            device_id_type=MESH,
        )

    barrier = pltpu.get_barrier_semaphore()
    for other in (nexts[0], nexts[1], sibling):
        pl.semaphore_signal(barrier, inc=1, device_id={"ctx": other}, device_id_type=MESH)
    pl.semaphore_wait(barrier, 3)

    sends = []
    sib_waits = []
    my_rows = pl.ds(pl.multiple_of(me * rows, rows), rows)
    sib_rows = pl.ds(pl.multiple_of(sibling * rows, rows), rows)
    for a in (0, 1):
        for direction in (0, 1):
            c = ring_copy(ins[a], me, a, direction, 1)
            c.start()
            sends.append(c)
    own = []
    for a in (0, 1):
        c = sib_copy(ins[a], outs[a].at[my_rows], a, 0)
        c.start()
        sends.append(c)
        sib_waits.append(sib_copy(outs[a].at[sib_rows], outs[a].at[sib_rows], a, 0))
        local = pltpu.make_async_copy(ins[a], outs[a].at[my_rows], own_sem.at[a])
        local.start()
        own.append(local)
    for hop in range(1, half_chips + 1):
        for a in (0, 1):
            for direction in (0, 1):
                step = hop if direction == 0 else -hop
                owner = device_at(pos - step)
                here = outs[a].at[piece(owner, direction, hop)]
                ring_copy(here, owner, a, direction, hop).wait_recv()
                if hop < half_chips:
                    onward = outs[a].at[piece(owner, direction, hop + 1)]
                    c = ring_copy(onward, owner, a, direction, hop + 1)
                    c.start()
                    sends.append(c)
                slot = 1 + 2 * (hop - 1) + direction
                c = sib_copy(here, here, a, slot)
                c.start()
                sends.append(c)
                other = owner + 1 - 2 * core
                there = outs[a].at[piece(other, direction, hop)]
                sib_waits.append(sib_copy(there, there, a, slot))
    for c in own:
        c.wait()
    for c in sib_waits:
        c.wait_recv()
    for c in sends:
        c.wait_send()


def ring_gather(x, g):
    n = lax.axis_size("ctx")
    hops = n // 4
    rows, width = x.shape
    out = jax.ShapeDtypeStruct((n * rows, width), x.dtype)
    return pl.pallas_call(
        functools.partial(ring_gather_kernel, n),
        out_shape=(out, out),
        in_specs=[pl.BlockSpec(memory_space=pl.ANY)] * 2,
        out_specs=(pl.BlockSpec(memory_space=pl.ANY),) * 2,
        scratch_shapes=[
            pltpu.SemaphoreType.DMA((2, hops, 2)),
            pltpu.SemaphoreType.DMA((2, hops, 2)),
            pltpu.SemaphoreType.DMA((1 + 2 * hops, 2)),
            pltpu.SemaphoreType.DMA((1 + 2 * hops, 2)),
            pltpu.SemaphoreType.DMA((2,)),
        ],
        compiler_params=pltpu.CompilerParams(collective_id=0, has_side_effects=True),
        cost_estimate=pl.CostEstimate(
            flops=0, bytes_accessed=4 * n * rows * width * 2, transcendentals=0
        ),
        name="ring_gather",
    )(x, g)


def dot_rows(a, b):
    return lax.dot_general(a, b, (((1,), (1,)), ((), ())), preferred_element_type=jnp.float32)


def query_kernel(q_ref, k_ref, v_ref, g_ref, open_ref, off_ref, qg_ref, lt_ref, rd_ref):
    keys = k_ref.shape[0]
    rows = q_ref.shape[0]
    key_pos = lax.broadcasted_iota(jnp.int32, (keys, rows), 0)
    query_pos = lax.broadcasted_iota(jnp.int32, (keys, rows), 1) + off_ref[0]
    allowed = (open_ref[...] > 0) & (key_pos <= query_pos)
    k, v, q, g = k_ref[...], v_ref[...], q_ref[...], g_ref[...]
    scores = jnp.where(allowed, dot_rows(k, q) * INV_ROOT, -jnp.inf)
    row_max = jnp.max(scores, axis=0, keepdims=True)
    log_total = row_max + jnp.log(jnp.sum(jnp.exp(scores - row_max), axis=0, keepdims=True))
    prob = jnp.exp(scores - log_total)
    prob_low = prob.astype(jnp.bfloat16)
    prob_grad = dot_rows(v, g)
    row_delta = jnp.sum(prob_low.astype(jnp.float32) * prob_grad, axis=0, keepdims=True)
    dscore = (prob * (prob_grad - row_delta)).astype(jnp.bfloat16)
    total = lax.dot_general(
        dscore, k, (((0,), (0,)), ((), ())), preferred_element_type=jnp.float32
    )
    qg_ref[...] = (total * INV_ROOT).astype(jnp.bfloat16)
    lt_ref[0] = log_total
    rd_ref[0] = row_delta


def query_side(q, k_all, v_all, g, key_open, offset):
    rows = q.shape[0]
    keys = k_all.shape[0]
    heads = q.shape[1] // HD
    return pl.pallas_call(
        query_kernel,
        grid=(heads,),
        out_shape=(
            jax.ShapeDtypeStruct(q.shape, jnp.bfloat16),
            jax.ShapeDtypeStruct((heads, 1, rows), jnp.float32),
            jax.ShapeDtypeStruct((heads, 1, rows), jnp.float32),
        ),
        in_specs=[
            pl.BlockSpec((rows, HD), lambda h: (0, h)),
            pl.BlockSpec((keys, HD), lambda h: (0, h)),
            pl.BlockSpec((keys, HD), lambda h: (0, h)),
            pl.BlockSpec((rows, HD), lambda h: (0, h)),
            pl.BlockSpec((keys, 1), lambda h: (0, 0)),
            pl.BlockSpec(memory_space=pltpu.SMEM),
        ],
        out_specs=(
            pl.BlockSpec((rows, HD), lambda h: (0, h)),
            pl.BlockSpec((1, 1, rows), lambda h: (h, 0, 0)),
            pl.BlockSpec((1, 1, rows), lambda h: (h, 0, 0)),
        ),
        compiler_params=pltpu.CompilerParams(vmem_limit_bytes=40 * 1024 * 1024),
        cost_estimate=pl.CostEstimate(
            flops=6 * heads * rows * keys * HD,
            bytes_accessed=4 * heads * keys * HD,
            transcendentals=2 * heads * rows * keys,
        ),
        name="query_side",
    )(q, k_all, v_all, g, key_open, offset)


def key_kernel(k_ref, v_ref, q_ref, g_ref, lt_ref, rd_ref, listed_ref, open_ref, off_ref, kg_ref, vg_ref):
    keys = k_ref.shape[0]
    queries = q_ref.shape[0]
    key_pos = lax.broadcasted_iota(jnp.int32, (keys, queries), 0) + off_ref[0]
    query_pos = lax.broadcasted_iota(jnp.int32, (keys, queries), 1)
    allowed = (listed_ref[...] > 0) & (open_ref[...] > 0) & (key_pos <= query_pos)
    k, v, q, g = k_ref[...], v_ref[...], q_ref[...], g_ref[...]
    scores = jnp.where(allowed, dot_rows(k, q) * INV_ROOT, -jnp.inf)
    prob = jnp.exp(scores - lt_ref[0])
    prob_low = prob.astype(jnp.bfloat16)
    prob_grad = dot_rows(v, g)
    dscore = (prob * (prob_grad - rd_ref[0])).astype(jnp.bfloat16)
    vg_ref[...] = jnp.dot(prob_low, g, preferred_element_type=jnp.float32).astype(jnp.bfloat16)
    kg_ref[...] = (jnp.dot(dscore, q, preferred_element_type=jnp.float32) * INV_ROOT).astype(
        jnp.bfloat16
    )


def key_side(k, v, q_all, g_all, log_total, row_delta, listed, key_open, offset):
    keys = k.shape[0]
    queries = q_all.shape[0]
    heads = k.shape[1] // HD
    small = pl.BlockSpec((keys, HD), lambda h: (0, h))
    large = pl.BlockSpec((queries, HD), lambda h: (0, h))
    stat = pl.BlockSpec((1, 1, queries), lambda h: (h, 0, 0))
    out = jax.ShapeDtypeStruct(k.shape, jnp.bfloat16)
    return pl.pallas_call(
        key_kernel,
        grid=(heads,),
        out_shape=(out, out),
        in_specs=[
            small,
            small,
            large,
            large,
            stat,
            stat,
            pl.BlockSpec((1, queries), lambda h: (0, 0)),
            pl.BlockSpec((keys, 1), lambda h: (0, 0)),
            pl.BlockSpec(memory_space=pltpu.SMEM),
        ],
        out_specs=(small, small),
        compiler_params=pltpu.CompilerParams(vmem_limit_bytes=40 * 1024 * 1024),
        cost_estimate=pl.CostEstimate(
            flops=8 * heads * keys * queries * HD,
            bytes_accessed=4 * heads * queries * HD,
            transcendentals=heads * keys * queries,
        ),
        name="key_side",
    )(k, v, q_all, g_all, log_total, row_delta, listed, key_open, offset)


def per_device(
    query_rows,
    key_rows,
    value_rows,
    block_lists,
    block_lengths,
    out_weight,
    expert_input,
    layer_grad,
    route_experts,
    route_weight,
    gate_weight,
    up_weight,
    down_weight,
):
    n = lax.axis_size("ctx")
    dp = lax.axis_size("dp")
    me = lax.axis_index("ctx")
    my_dp = lax.axis_index("dp")
    rows = query_rows.shape[1]
    seq_len = rows * n
    blocks = seq_len // BLK
    width = expert_input.shape[2]

    experts = jnp.arange(n, dtype=jnp.int32)
    matches = route_experts[0].T[None, :, :] == experts[:, None, None]
    coef_here = jnp.sum(jnp.where(matches, route_weight[0].T[None, :, :], 0.0), axis=1)
    coef_all = lax.all_gather(coef_here, "ctx", axis=0)
    coef = lax.dynamic_index_in_dim(coef_all, me, axis=1, keepdims=False)

    k_all = lax.all_gather(key_rows[0], "ctx", axis=0, tiled=True)
    v_all = lax.all_gather(value_rows[0], "ctx", axis=0, tiled=True)
    q_all = lax.all_gather(query_rows[0], "ctx", axis=0, tiled=True)
    x_all, g_all = ring_gather(expert_input[0], layer_grad[0])

    capacity = min(rows, rows * TOPK * 4 // (3 * n))
    present = coef > 0.0
    rank = jnp.cumsum(present.astype(jnp.int32), axis=1) - 1
    slots = jnp.arange(capacity, dtype=jnp.int32)
    chosen = present[:, None, :] & (rank[:, None, :] == slots[None, :, None])
    onehot = chosen.astype(jnp.bfloat16)
    slot_coef = jnp.sum(jnp.where(chosen, coef[:, None, :], 0.0), axis=2)
    picked = jnp.einsum(
        "ics,isd->icd", onehot, x_all.reshape(n, rows, width), preferred_element_type=jnp.float32
    ).astype(jnp.bfloat16)
    picked_grad = jnp.einsum(
        "ics,isd->icd", onehot, g_all.reshape(n, rows, width), preferred_element_type=jnp.float32
    )
    scaled = (slot_coef[:, :, None] * picked_grad).astype(jnp.bfloat16)
    tokens = picked.reshape(n * capacity, width)
    grads = scaled.reshape(n * capacity, width)

    gate_pre = jnp.dot(tokens, gate_weight[0], preferred_element_type=jnp.float32)
    up_pre = jnp.dot(tokens, up_weight[0], preferred_element_type=jnp.float32)
    hidden_grad = jnp.dot(grads, down_weight[0], preferred_element_type=jnp.float32)
    gate_sig = jax.nn.sigmoid(gate_pre)
    gate_act = gate_pre * gate_sig
    hidden = (gate_act * up_pre).astype(jnp.bfloat16)
    gate_delta = (hidden_grad * up_pre * gate_sig * (1.0 + gate_pre * (1.0 - gate_sig))).astype(
        jnp.bfloat16
    )
    up_delta = (hidden_grad * gate_act).astype(jnp.bfloat16)

    def partial(a, b):
        return lax.dot_general(
            a, b, (((0,), (0,)), ((), ())), preferred_element_type=jnp.float32
        ).astype(jnp.bfloat16)

    pairs = ((grads, hidden), (tokens, gate_delta), (tokens, up_delta))
    if dp == 2:
        half = width // 2
        swap = [(0, 1), (1, 0)]
        arrived = [
            lax.ppermute(
                partial(lax.dynamic_slice_in_dim(a, (1 - my_dp) * half, half, 1), b), "dp", swap
            )
            for a, b in pairs
        ]
        sums = [
            partial(lax.dynamic_slice_in_dim(a, my_dp * half, half, 1), b).astype(jnp.float32)
            + r.astype(jnp.float32)
            for (a, b), r in zip(pairs, arrived)
        ]
    else:
        sums = [
            lax.psum_scatter(partial(a, b), "dp", scatter_dimension=0, tiled=True).astype(
                jnp.float32
            )
            for a, b in pairs
        ]
    down_grad, gate_grad, up_grad = (s[None] for s in sums)

    out_all = lax.dot_general(
        g_all, out_weight, (((1,), (1,)), ((), ())), preferred_element_type=jnp.float32
    ).astype(jnp.bfloat16)
    out_here = lax.dynamic_slice_in_dim(out_all, me * rows, rows, 0)
    lists = block_lists[0]
    lengths = block_lengths[0]
    block_ids = jnp.arange(blocks, dtype=jnp.int32)
    offsets = jnp.arange(BLK, dtype=jnp.int32)
    valid = offsets[None, :] < lengths[:, None]
    my_list = lax.dynamic_index_in_dim(lists, me, 0, keepdims=False)
    my_blocks = jnp.any(my_list[None, :] == block_ids[:, None], axis=1)
    open_all = (my_blocks[:, None] & valid).astype(jnp.int32).reshape(seq_len, 1)
    offset = jnp.reshape(me * rows, (1,)).astype(jnp.int32)
    query_grad, log_total, row_delta = query_side(
        query_rows[0], k_all, v_all, out_here, open_all, offset
    )
    stats = jnp.stack([log_total[:, 0], row_delta[:, 0]])
    stats_all = lax.all_gather(stats, "ctx", axis=2, tiled=True)
    lists_me = jnp.any(lists == me, axis=1)
    listed = jnp.broadcast_to(lists_me[:, None], (blocks, BLK)).astype(jnp.int32)
    my_open = lax.dynamic_index_in_dim(valid, me, 0, keepdims=False).astype(jnp.int32)
    key_grad, value_grad = key_side(
        key_rows[0],
        value_rows[0],
        q_all,
        out_all,
        stats_all[0][:, None, :],
        stats_all[1][:, None, :],
        listed.reshape(1, seq_len),
        my_open.reshape(BLK, 1),
        offset,
    )
    return (query_grad[None], key_grad[None], value_grad[None], gate_grad, up_grad, down_grad)


def solution(mesh):
    in_specs = (
        P("dp", "ctx", None),
        P("dp", "ctx", None),
        P("dp", "ctx", None),
        P("dp", None, None),
        P("dp", None),
        P(),
        P("dp", "ctx", None),
        P("dp", "ctx", None),
        P("dp", "ctx", None),
        P("dp", "ctx", None),
        P("ctx", None, None),
        P("ctx", None, None),
        P("ctx", None, None),
    )
    out_specs = (
        P("dp", "ctx", None),
        P("dp", "ctx", None),
        P("dp", "ctx", None),
        P("ctx", "dp", None),
        P("ctx", "dp", None),
        P("ctx", "dp", None),
    )
    return jax.shard_map(
        per_device, mesh=mesh, in_specs=in_specs, out_specs=out_specs, check_vma=False
    )
```

```python
import functools
import math

import jax
import jax.numpy as jnp
from jax import lax
from jax.experimental import pallas as pl
from jax.experimental.pallas import tpu as pltpu
from jax.sharding import PartitionSpec as P

HEADS = 8
HD = 128
TOPK = 6
BLK = 128
INV_ROOT = 1.0 / math.sqrt(HD)
MESH = pl.DeviceIdType.MESH


def ring_gather_kernel(n, count, *refs):
    chips = n // 2
    half_chips = chips // 2
    ins, outs = refs[:count], refs[count : 2 * count]
    ring_send, ring_recv, sib_send, sib_recv, own_sem = refs[2 * count :]
    me = lax.axis_index("ctx")
    core = me % 2
    chip = me // 2
    z, y = chip // 2, chip % 2
    pos = z + y * (chips - 1 - 2 * z)

    def device_at(p):
        p = (p + 2 * chips) % chips
        hi = p // half_chips
        return 2 * (2 * p + hi * (2 * chips - 1 - 4 * p)) + core

    sibling = me + 1 - 2 * core
    nexts = (device_at(pos + 1), device_at(pos - 1))

    def piece(owner, a, direction, hop):
        rows = ins[a].shape[0]
        if hop < half_chips:
            return pl.ds(pl.multiple_of(owner * rows, rows), rows)
        part = rows // 2
        return pl.ds(pl.multiple_of(owner * rows + direction * part, part), part)

    def ring_copy(src, owner, a, direction, hop):
        return pltpu.make_async_remote_copy(
            src_ref=src,
            dst_ref=outs[a].at[piece(owner, a, direction, hop)],
            send_sem=ring_send.at[direction, hop - 1, a],
            recv_sem=ring_recv.at[direction, hop - 1, a],
            device_id={"ctx": nexts[direction]},
            device_id_type=MESH,
        )

    def sib_copy(src, dst, a, slot):
        return pltpu.make_async_remote_copy(
            src_ref=src,
            dst_ref=dst,
            send_sem=sib_send.at[slot, a],
            recv_sem=sib_recv.at[slot, a],
            device_id={"ctx": sibling},
            device_id_type=MESH,
        )

    barrier = pltpu.get_barrier_semaphore()
    for other in (nexts[0], nexts[1], sibling):
        pl.semaphore_signal(barrier, inc=1, device_id={"ctx": other}, device_id_type=MESH)
    pl.semaphore_wait(barrier, 3)

    sends = []
    sib_waits = []
    for a in range(count):
        for direction in (0, 1):
            c = ring_copy(ins[a], me, a, direction, 1)
            c.start()
            sends.append(c)
    own = []
    for a in range(count):
        c = sib_copy(ins[a], outs[a].at[piece(me, a, 0, 1)], a, 0)
        c.start()
        sends.append(c)
        sib_waits.append(sib_copy(outs[a].at[piece(sibling, a, 0, 1)], outs[a].at[piece(sibling, a, 0, 1)], a, 0))
        local = pltpu.make_async_copy(ins[a], outs[a].at[piece(me, a, 0, 1)], own_sem.at[a])
        local.start()
        own.append(local)
    for hop in range(1, half_chips + 1):
        for a in range(count):
            for direction in (0, 1):
                step = hop if direction == 0 else -hop
                owner = device_at(pos - step)
                here = outs[a].at[piece(owner, a, direction, hop)]
                ring_copy(here, owner, a, direction, hop).wait_recv()
                if hop < half_chips:
                    onward = outs[a].at[piece(owner, a, direction, hop + 1)]
                    c = ring_copy(onward, owner, a, direction, hop + 1)
                    c.start()
                    sends.append(c)
                slot = 1 + 2 * (hop - 1) + direction
                c = sib_copy(here, here, a, slot)
                c.start()
                sends.append(c)
                other = owner + 1 - 2 * core
                there = outs[a].at[piece(other, a, direction, hop)]
                sib_waits.append(sib_copy(there, there, a, slot))
    for c in own:
        c.wait()
    for c in sib_waits:
        c.wait_recv()
    for c in sends:
        c.wait_send()


def ring_gather(arrays, collective_id):
    n = lax.axis_size("ctx")
    hops = n // 4
    count = len(arrays)
    anywhere = pl.BlockSpec(memory_space=pl.ANY)
    return pl.pallas_call(
        functools.partial(ring_gather_kernel, n, count),
        out_shape=tuple(
            jax.ShapeDtypeStruct((n * a.shape[0], a.shape[1]), a.dtype) for a in arrays
        ),
        in_specs=[anywhere] * count,
        out_specs=(anywhere,) * count,
        scratch_shapes=[
            pltpu.SemaphoreType.DMA((2, hops, count)),
            pltpu.SemaphoreType.DMA((2, hops, count)),
            pltpu.SemaphoreType.DMA((1 + 2 * hops, count)),
            pltpu.SemaphoreType.DMA((1 + 2 * hops, count)),
            pltpu.SemaphoreType.DMA((count,)),
        ],
        compiler_params=pltpu.CompilerParams(collective_id=collective_id, has_side_effects=True),
        cost_estimate=pl.CostEstimate(
            flops=0,
            bytes_accessed=sum(4 * n * a.size * a.dtype.itemsize for a in arrays),
            transcendentals=0,
        ),
        name="ring_gather_%d" % collective_id,
    )(*arrays)


def dot_rows(a, b):
    return lax.dot_general(a, b, (((1,), (1,)), ((), ())), preferred_element_type=jnp.float32)


def query_kernel(q_ref, k_ref, v_ref, g_ref, open_ref, off_ref, qg_ref, lt_ref, rd_ref):
    keys = k_ref.shape[0]
    rows = q_ref.shape[0]
    key_pos = lax.broadcasted_iota(jnp.int32, (keys, rows), 0)
    query_pos = lax.broadcasted_iota(jnp.int32, (keys, rows), 1) + off_ref[0]
    allowed = (open_ref[...] > 0) & (key_pos <= query_pos)
    k, v, q, g = k_ref[...], v_ref[...], q_ref[...], g_ref[...]
    scores = jnp.where(allowed, dot_rows(k, q) * INV_ROOT, -jnp.inf)
    row_max = jnp.max(scores, axis=0, keepdims=True)
    log_total = row_max + jnp.log(jnp.sum(jnp.exp(scores - row_max), axis=0, keepdims=True))
    prob = jnp.exp(scores - log_total)
    prob_low = prob.astype(jnp.bfloat16)
    prob_grad = dot_rows(v, g)
    row_delta = jnp.sum(prob_low.astype(jnp.float32) * prob_grad, axis=0, keepdims=True)
    dscore = (prob * (prob_grad - row_delta)).astype(jnp.bfloat16)
    total = lax.dot_general(
        dscore, k, (((0,), (0,)), ((), ())), preferred_element_type=jnp.float32
    )
    qg_ref[...] = (total * INV_ROOT).astype(jnp.bfloat16)
    lt_ref[0] = log_total
    rd_ref[0] = row_delta


def query_side(q, k_all, v_all, g, key_open, offset):
    rows = q.shape[0]
    keys = k_all.shape[0]
    heads = q.shape[1] // HD
    return pl.pallas_call(
        query_kernel,
        grid=(heads,),
        out_shape=(
            jax.ShapeDtypeStruct(q.shape, jnp.bfloat16),
            jax.ShapeDtypeStruct((heads, 1, rows), jnp.float32),
            jax.ShapeDtypeStruct((heads, 1, rows), jnp.float32),
        ),
        in_specs=[
            pl.BlockSpec((rows, HD), lambda h: (0, h)),
            pl.BlockSpec((keys, HD), lambda h: (0, h)),
            pl.BlockSpec((keys, HD), lambda h: (0, h)),
            pl.BlockSpec((rows, HD), lambda h: (0, h)),
            pl.BlockSpec((keys, 1), lambda h: (0, 0)),
            pl.BlockSpec(memory_space=pltpu.SMEM),
        ],
        out_specs=(
            pl.BlockSpec((rows, HD), lambda h: (0, h)),
            pl.BlockSpec((1, 1, rows), lambda h: (h, 0, 0)),
            pl.BlockSpec((1, 1, rows), lambda h: (h, 0, 0)),
        ),
        compiler_params=pltpu.CompilerParams(vmem_limit_bytes=40 * 1024 * 1024),
        cost_estimate=pl.CostEstimate(
            flops=6 * heads * rows * keys * HD,
            bytes_accessed=4 * heads * keys * HD,
            transcendentals=2 * heads * rows * keys,
        ),
        name="query_side",
    )(q, k_all, v_all, g, key_open, offset)


def key_kernel(k_ref, v_ref, q_ref, g_ref, lt_ref, rd_ref, listed_ref, open_ref, off_ref, kg_ref, vg_ref):
    keys = k_ref.shape[0]
    queries = q_ref.shape[0]
    key_pos = lax.broadcasted_iota(jnp.int32, (keys, queries), 0) + off_ref[0]
    query_pos = lax.broadcasted_iota(jnp.int32, (keys, queries), 1)
    allowed = (listed_ref[...] > 0) & (open_ref[...] > 0) & (key_pos <= query_pos)
    k, v, q, g = k_ref[...], v_ref[...], q_ref[...], g_ref[...]
    scores = jnp.where(allowed, dot_rows(k, q) * INV_ROOT, -jnp.inf)
    prob = jnp.exp(scores - lt_ref[0])
    prob_low = prob.astype(jnp.bfloat16)
    prob_grad = dot_rows(v, g)
    dscore = (prob * (prob_grad - rd_ref[0])).astype(jnp.bfloat16)
    vg_ref[...] = jnp.dot(prob_low, g, preferred_element_type=jnp.float32).astype(jnp.bfloat16)
    kg_ref[...] = (jnp.dot(dscore, q, preferred_element_type=jnp.float32) * INV_ROOT).astype(
        jnp.bfloat16
    )


def key_side(k, v, q_all, g_all, log_total, row_delta, listed, key_open, offset):
    keys = k.shape[0]
    queries = q_all.shape[0]
    heads = k.shape[1] // HD
    small = pl.BlockSpec((keys, HD), lambda h: (0, h))
    large = pl.BlockSpec((queries, HD), lambda h: (0, h))
    stat = pl.BlockSpec((1, 1, queries), lambda h: (h, 0, 0))
    out = jax.ShapeDtypeStruct(k.shape, jnp.bfloat16)
    return pl.pallas_call(
        key_kernel,
        grid=(heads,),
        out_shape=(out, out),
        in_specs=[
            small,
            small,
            large,
            large,
            stat,
            stat,
            pl.BlockSpec((1, queries), lambda h: (0, 0)),
            pl.BlockSpec((keys, 1), lambda h: (0, 0)),
            pl.BlockSpec(memory_space=pltpu.SMEM),
        ],
        out_specs=(small, small),
        compiler_params=pltpu.CompilerParams(vmem_limit_bytes=40 * 1024 * 1024),
        cost_estimate=pl.CostEstimate(
            flops=8 * heads * keys * queries * HD,
            bytes_accessed=4 * heads * queries * HD,
            transcendentals=heads * keys * queries,
        ),
        name="key_side",
    )(k, v, q_all, g_all, log_total, row_delta, listed, key_open, offset)


def per_device(
    query_rows,
    key_rows,
    value_rows,
    block_lists,
    block_lengths,
    out_weight,
    expert_input,
    layer_grad,
    route_experts,
    route_weight,
    gate_weight,
    up_weight,
    down_weight,
):
    n = lax.axis_size("ctx")
    dp = lax.axis_size("dp")
    me = lax.axis_index("ctx")
    my_dp = lax.axis_index("dp")
    rows = query_rows.shape[1]
    seq_len = rows * n
    blocks = seq_len // BLK
    width = expert_input.shape[2]

    experts = jnp.arange(n, dtype=jnp.int32)
    matches = route_experts[0].T[None, :, :] == experts[:, None, None]
    coef_here = jnp.sum(jnp.where(matches, route_weight[0].T[None, :, :], 0.0), axis=1)
    coef_all, x_all, g_all = ring_gather((coef_here, expert_input[0], layer_grad[0]), 0)
    coef = lax.dynamic_index_in_dim(coef_all.reshape(n, n, rows), me, axis=1, keepdims=False)

    capacity = min(rows, rows * TOPK * 4 // (3 * n))
    present = coef > 0.0
    rank = jnp.cumsum(present.astype(jnp.int32), axis=1) - 1
    slots = jnp.arange(capacity, dtype=jnp.int32)
    chosen = present[:, None, :] & (rank[:, None, :] == slots[None, :, None])
    onehot = chosen.astype(jnp.bfloat16)
    slot_coef = jnp.sum(jnp.where(chosen, coef[:, None, :], 0.0), axis=2)
    picked = jnp.einsum(
        "ics,isd->icd", onehot, x_all.reshape(n, rows, width), preferred_element_type=jnp.float32
    ).astype(jnp.bfloat16)
    picked_grad = jnp.einsum(
        "ics,isd->icd", onehot, g_all.reshape(n, rows, width), preferred_element_type=jnp.float32
    )
    scaled = (slot_coef[:, :, None] * picked_grad).astype(jnp.bfloat16)
    tokens = picked.reshape(n * capacity, width)
    grads = scaled.reshape(n * capacity, width)

    gate_pre = jnp.dot(tokens, gate_weight[0], preferred_element_type=jnp.float32)
    up_pre = jnp.dot(tokens, up_weight[0], preferred_element_type=jnp.float32)
    hidden_grad = jnp.dot(grads, down_weight[0], preferred_element_type=jnp.float32)
    gate_sig = jax.nn.sigmoid(gate_pre)
    gate_act = gate_pre * gate_sig
    hidden = (gate_act * up_pre).astype(jnp.bfloat16)
    gate_delta = (hidden_grad * up_pre * gate_sig * (1.0 + gate_pre * (1.0 - gate_sig))).astype(
        jnp.bfloat16
    )
    up_delta = (hidden_grad * gate_act).astype(jnp.bfloat16)

    def partial(a, b):
        return lax.dot_general(
            a, b, (((0,), (0,)), ((), ())), preferred_element_type=jnp.float32
        ).astype(jnp.bfloat16)

    pairs = ((grads, hidden), (tokens, gate_delta), (tokens, up_delta))
    if dp == 2:
        half = width // 2
        swap = [(0, 1), (1, 0)]
        leaving = [
            partial(lax.dynamic_slice_in_dim(a, (1 - my_dp) * half, half, 1), b) for a, b in pairs
        ]
        arrived = [lax.ppermute(a, "dp", swap) for a in leaving]
    else:
        leaving = [partial(a, b) for a, b in pairs]
        arrived = [lax.psum_scatter(a, "dp", scatter_dimension=0, tiled=True) for a in leaving]
    key_in, value_in, query_in, _ = lax.optimization_barrier(
        (key_rows[0], value_rows[0], query_rows[0], leaving)
    )
    k_all, v_all, q_all = ring_gather((key_in, value_in, query_in), 1)

    out_all = lax.dot_general(
        g_all, out_weight, (((1,), (1,)), ((), ())), preferred_element_type=jnp.float32
    ).astype(jnp.bfloat16)
    out_here = lax.dynamic_slice_in_dim(out_all, me * rows, rows, 0)
    lists = block_lists[0]
    lengths = block_lengths[0]
    block_ids = jnp.arange(blocks, dtype=jnp.int32)
    offsets = jnp.arange(BLK, dtype=jnp.int32)
    valid = offsets[None, :] < lengths[:, None]
    my_list = lax.dynamic_index_in_dim(lists, me, 0, keepdims=False)
    my_blocks = jnp.any(my_list[None, :] == block_ids[:, None], axis=1)
    open_all = (my_blocks[:, None] & valid).astype(jnp.int32).reshape(seq_len, 1)
    offset = jnp.reshape(me * rows, (1,)).astype(jnp.int32)
    query_grad, log_total, row_delta = query_side(
        query_rows[0], k_all, v_all, out_here, open_all, offset
    )
    stats = jnp.stack([log_total[:, 0], row_delta[:, 0]])
    stats_all = lax.all_gather(stats, "ctx", axis=2, tiled=True)
    lists_me = jnp.any(lists == me, axis=1)
    listed = jnp.broadcast_to(lists_me[:, None], (blocks, BLK)).astype(jnp.int32)
    my_open = lax.dynamic_index_in_dim(valid, me, 0, keepdims=False).astype(jnp.int32)
    key_grad, value_grad = key_side(
        key_rows[0],
        value_rows[0],
        q_all,
        out_all,
        stats_all[0][:, None, :],
        stats_all[1][:, None, :],
        listed.reshape(1, seq_len),
        my_open.reshape(BLK, 1),
        offset,
    )
    if dp == 2:
        key_grad, right = lax.optimization_barrier((key_grad, [b for _, b in pairs]))
        sums = [
            partial(lax.dynamic_slice_in_dim(a, my_dp * half, half, 1), b).astype(jnp.float32)
            + r.astype(jnp.float32)
            for (a, _), b, r in zip(pairs, right, arrived)
        ]
    else:
        sums = [r.astype(jnp.float32) for r in arrived]
    down_grad, gate_grad, up_grad = (s[None] for s in sums)
    return (query_grad[None], key_grad[None], value_grad[None], gate_grad, up_grad, down_grad)


def solution(mesh):
    in_specs = (
        P("dp", "ctx", None),
        P("dp", "ctx", None),
        P("dp", "ctx", None),
        P("dp", None, None),
        P("dp", None),
        P(),
        P("dp", "ctx", None),
        P("dp", "ctx", None),
        P("dp", "ctx", None),
        P("dp", "ctx", None),
        P("ctx", None, None),
        P("ctx", None, None),
        P("ctx", None, None),
    )
    out_specs = (
        P("dp", "ctx", None),
        P("dp", "ctx", None),
        P("dp", "ctx", None),
        P("ctx", "dp", None),
        P("ctx", "dp", None),
        P("ctx", "dp", None),
    )
    return jax.shard_map(
        per_device, mesh=mesh, in_specs=in_specs, out_specs=out_specs, check_vma=False
    )
```

```python
import functools
import math

import jax
import jax.numpy as jnp
from jax import lax
from jax.experimental import pallas as pl
from jax.experimental.pallas import tpu as pltpu
from jax.sharding import PartitionSpec as P

HEADS = 8
HD = 128
TOPK = 6
BLK = 128
INV_ROOT = 1.0 / math.sqrt(HD)
MESH = pl.DeviceIdType.MESH


def ring_gather_kernel(n, count, *refs):
    chips = n // 2
    half_chips = chips // 2
    ins, outs = refs[:count], refs[count : 2 * count]
    ring_send, ring_recv, sib_send, sib_recv, own_sem = refs[2 * count :]
    me = lax.axis_index("ctx")
    core = me % 2
    chip = me // 2
    z, y = chip // 2, chip % 2
    pos = z + y * (chips - 1 - 2 * z)

    def device_at(p):
        p = (p + 2 * chips) % chips
        hi = p // half_chips
        return 2 * (2 * p + hi * (2 * chips - 1 - 4 * p)) + core

    sibling = me + 1 - 2 * core
    nexts = (device_at(pos + 1), device_at(pos - 1))

    def piece(owner, a, direction, hop):
        rows = ins[a].shape[0]
        if hop < half_chips:
            return pl.ds(pl.multiple_of(owner * rows, rows), rows)
        part = rows // 2
        return pl.ds(pl.multiple_of(owner * rows + direction * part, part), part)

    def ring_copy(src, owner, a, direction, hop):
        return pltpu.make_async_remote_copy(
            src_ref=src,
            dst_ref=outs[a].at[piece(owner, a, direction, hop)],
            send_sem=ring_send.at[direction, hop - 1, a],
            recv_sem=ring_recv.at[direction, hop - 1, a],
            device_id={"ctx": nexts[direction]},
            device_id_type=MESH,
        )

    def sib_copy(src, dst, a, slot):
        return pltpu.make_async_remote_copy(
            src_ref=src,
            dst_ref=dst,
            send_sem=sib_send.at[slot, a],
            recv_sem=sib_recv.at[slot, a],
            device_id={"ctx": sibling},
            device_id_type=MESH,
        )

    barrier = pltpu.get_barrier_semaphore()
    for other in (nexts[0], nexts[1], sibling):
        pl.semaphore_signal(barrier, inc=1, device_id={"ctx": other}, device_id_type=MESH)
    pl.semaphore_wait(barrier, 3)

    sends = []
    sib_waits = []
    for a in range(count):
        for direction in (0, 1):
            c = ring_copy(ins[a], me, a, direction, 1)
            c.start()
            sends.append(c)
    own = []
    for a in range(count):
        c = sib_copy(ins[a], outs[a].at[piece(me, a, 0, 1)], a, 0)
        c.start()
        sends.append(c)
        sib_waits.append(sib_copy(outs[a].at[piece(sibling, a, 0, 1)], outs[a].at[piece(sibling, a, 0, 1)], a, 0))
        local = pltpu.make_async_copy(ins[a], outs[a].at[piece(me, a, 0, 1)], own_sem.at[a])
        local.start()
        own.append(local)
    for hop in range(1, half_chips + 1):
        for a in range(count):
            for direction in (0, 1):
                step = hop if direction == 0 else -hop
                owner = device_at(pos - step)
                here = outs[a].at[piece(owner, a, direction, hop)]
                ring_copy(here, owner, a, direction, hop).wait_recv()
                if hop < half_chips:
                    onward = outs[a].at[piece(owner, a, direction, hop + 1)]
                    c = ring_copy(onward, owner, a, direction, hop + 1)
                    c.start()
                    sends.append(c)
                slot = 1 + 2 * (hop - 1) + direction
                c = sib_copy(here, here, a, slot)
                c.start()
                sends.append(c)
                other = owner + 1 - 2 * core
                there = outs[a].at[piece(other, a, direction, hop)]
                sib_waits.append(sib_copy(there, there, a, slot))
    for c in own:
        c.wait()
    for c in sib_waits:
        c.wait_recv()
    for c in sends:
        c.wait_send()


def ring_gather(arrays, collective_id):
    n = lax.axis_size("ctx")
    hops = n // 4
    count = len(arrays)
    anywhere = pl.BlockSpec(memory_space=pl.ANY)
    return pl.pallas_call(
        functools.partial(ring_gather_kernel, n, count),
        out_shape=tuple(
            jax.ShapeDtypeStruct((n * a.shape[0], a.shape[1]), a.dtype) for a in arrays
        ),
        in_specs=[anywhere] * count,
        out_specs=(anywhere,) * count,
        scratch_shapes=[
            pltpu.SemaphoreType.DMA((2, hops, count)),
            pltpu.SemaphoreType.DMA((2, hops, count)),
            pltpu.SemaphoreType.DMA((1 + 2 * hops, count)),
            pltpu.SemaphoreType.DMA((1 + 2 * hops, count)),
            pltpu.SemaphoreType.DMA((count,)),
        ],
        compiler_params=pltpu.CompilerParams(collective_id=collective_id, has_side_effects=True),
        cost_estimate=pl.CostEstimate(
            flops=0,
            bytes_accessed=sum(4 * n * a.size * a.dtype.itemsize for a in arrays),
            transcendentals=0,
        ),
        name="ring_gather_%d" % collective_id,
    )(*arrays)


def dot_rows(a, b):
    return lax.dot_general(a, b, (((1,), (1,)), ((), ())), preferred_element_type=jnp.float32)


def query_kernel(q_ref, k_ref, v_ref, g_ref, open_ref, off_ref, qg_ref, lt_ref, rd_ref):
    keys = k_ref.shape[0]
    rows = q_ref.shape[0]
    key_pos = lax.broadcasted_iota(jnp.int32, (keys, rows), 0)
    query_pos = lax.broadcasted_iota(jnp.int32, (keys, rows), 1) + off_ref[0]
    allowed = (open_ref[...] > 0) & (key_pos <= query_pos)
    k, v, q, g = k_ref[...], v_ref[...], q_ref[...], g_ref[...]
    scores = jnp.where(allowed, dot_rows(k, q) * INV_ROOT, -jnp.inf)
    row_max = jnp.max(scores, axis=0, keepdims=True)
    log_total = row_max + jnp.log(jnp.sum(jnp.exp(scores - row_max), axis=0, keepdims=True))
    prob = jnp.exp(scores - log_total)
    prob_low = prob.astype(jnp.bfloat16)
    prob_grad = dot_rows(v, g)
    row_delta = jnp.sum(prob_low.astype(jnp.float32) * prob_grad, axis=0, keepdims=True)
    dscore = (prob * (prob_grad - row_delta)).astype(jnp.bfloat16)
    total = lax.dot_general(
        dscore, k, (((0,), (0,)), ((), ())), preferred_element_type=jnp.float32
    )
    qg_ref[...] = (total * INV_ROOT).astype(jnp.bfloat16)
    lt_ref[0] = log_total
    rd_ref[0] = row_delta


def query_side(q, k_all, v_all, g, key_open, offset):
    rows = q.shape[0]
    keys = k_all.shape[0]
    heads = q.shape[1] // HD
    return pl.pallas_call(
        query_kernel,
        grid=(heads,),
        out_shape=(
            jax.ShapeDtypeStruct(q.shape, jnp.bfloat16),
            jax.ShapeDtypeStruct((heads, 1, rows), jnp.float32),
            jax.ShapeDtypeStruct((heads, 1, rows), jnp.float32),
        ),
        in_specs=[
            pl.BlockSpec((rows, HD), lambda h: (0, h)),
            pl.BlockSpec((keys, HD), lambda h: (0, h)),
            pl.BlockSpec((keys, HD), lambda h: (0, h)),
            pl.BlockSpec((rows, HD), lambda h: (0, h)),
            pl.BlockSpec((keys, 1), lambda h: (0, 0)),
            pl.BlockSpec(memory_space=pltpu.SMEM),
        ],
        out_specs=(
            pl.BlockSpec((rows, HD), lambda h: (0, h)),
            pl.BlockSpec((1, 1, rows), lambda h: (h, 0, 0)),
            pl.BlockSpec((1, 1, rows), lambda h: (h, 0, 0)),
        ),
        compiler_params=pltpu.CompilerParams(vmem_limit_bytes=40 * 1024 * 1024),
        cost_estimate=pl.CostEstimate(
            flops=6 * heads * rows * keys * HD,
            bytes_accessed=4 * heads * keys * HD,
            transcendentals=2 * heads * rows * keys,
        ),
        name="query_side",
    )(q, k_all, v_all, g, key_open, offset)


def key_kernel(k_ref, v_ref, q_ref, g_ref, lt_ref, rd_ref, listed_ref, open_ref, off_ref, kg_ref, vg_ref):
    keys = k_ref.shape[0]
    queries = q_ref.shape[0]
    key_pos = lax.broadcasted_iota(jnp.int32, (keys, queries), 0) + off_ref[0]
    query_pos = lax.broadcasted_iota(jnp.int32, (keys, queries), 1)
    allowed = (listed_ref[...] > 0) & (open_ref[...] > 0) & (key_pos <= query_pos)
    k, v, q, g = k_ref[...], v_ref[...], q_ref[...], g_ref[...]
    scores = jnp.where(allowed, dot_rows(k, q) * INV_ROOT, -jnp.inf)
    prob = jnp.exp(scores - lt_ref[0])
    prob_low = prob.astype(jnp.bfloat16)
    prob_grad = dot_rows(v, g)
    dscore = (prob * (prob_grad - rd_ref[0])).astype(jnp.bfloat16)
    vg_ref[...] = jnp.dot(prob_low, g, preferred_element_type=jnp.float32).astype(jnp.bfloat16)
    kg_ref[...] = (jnp.dot(dscore, q, preferred_element_type=jnp.float32) * INV_ROOT).astype(
        jnp.bfloat16
    )


def key_side(k, v, q_all, g_all, log_total, row_delta, listed, key_open, offset):
    keys = k.shape[0]
    queries = q_all.shape[0]
    heads = k.shape[1] // HD
    small = pl.BlockSpec((keys, HD), lambda h: (0, h))
    large = pl.BlockSpec((queries, HD), lambda h: (0, h))
    stat = pl.BlockSpec((1, 1, queries), lambda h: (h, 0, 0))
    out = jax.ShapeDtypeStruct(k.shape, jnp.bfloat16)
    return pl.pallas_call(
        key_kernel,
        grid=(heads,),
        out_shape=(out, out),
        in_specs=[
            small,
            small,
            large,
            large,
            stat,
            stat,
            pl.BlockSpec((1, queries), lambda h: (0, 0)),
            pl.BlockSpec((keys, 1), lambda h: (0, 0)),
            pl.BlockSpec(memory_space=pltpu.SMEM),
        ],
        out_specs=(small, small),
        compiler_params=pltpu.CompilerParams(vmem_limit_bytes=40 * 1024 * 1024),
        cost_estimate=pl.CostEstimate(
            flops=8 * heads * keys * queries * HD,
            bytes_accessed=4 * heads * queries * HD,
            transcendentals=heads * keys * queries,
        ),
        name="key_side",
    )(k, v, q_all, g_all, log_total, row_delta, listed, key_open, offset)


def per_device(
    query_rows,
    key_rows,
    value_rows,
    block_lists,
    block_lengths,
    out_weight,
    expert_input,
    layer_grad,
    route_experts,
    route_weight,
    gate_weight,
    up_weight,
    down_weight,
):
    n = lax.axis_size("ctx")
    dp = lax.axis_size("dp")
    me = lax.axis_index("ctx")
    my_dp = lax.axis_index("dp")
    rows = query_rows.shape[1]
    seq_len = rows * n
    blocks = seq_len // BLK
    width = expert_input.shape[2]

    experts = jnp.arange(n, dtype=jnp.int32)
    matches = route_experts[0].T[None, :, :] == experts[:, None, None]
    coef_here = jnp.sum(jnp.where(matches, route_weight[0].T[None, :, :], 0.0), axis=1)
    coef_all, x_all, g_all = ring_gather((coef_here, expert_input[0], layer_grad[0]), 0)
    query_in, coef_all = lax.optimization_barrier((query_rows[0], coef_all))
    q_all = lax.all_gather(query_in, "ctx", axis=0, tiled=True)
    coef = lax.dynamic_index_in_dim(coef_all.reshape(n, n, rows), me, axis=1, keepdims=False)

    capacity = min(rows, rows * TOPK * 4 // (3 * n))
    present = coef > 0.0
    rank = jnp.cumsum(present.astype(jnp.int32), axis=1) - 1
    slots = jnp.arange(capacity, dtype=jnp.int32)
    chosen = present[:, None, :] & (rank[:, None, :] == slots[None, :, None])
    onehot = chosen.astype(jnp.bfloat16)
    slot_coef = jnp.sum(jnp.where(chosen, coef[:, None, :], 0.0), axis=2)
    picked = jnp.einsum(
        "ics,isd->icd", onehot, x_all.reshape(n, rows, width), preferred_element_type=jnp.float32
    ).astype(jnp.bfloat16)
    picked_grad = jnp.einsum(
        "ics,isd->icd", onehot, g_all.reshape(n, rows, width), preferred_element_type=jnp.float32
    )
    scaled = (slot_coef[:, :, None] * picked_grad).astype(jnp.bfloat16)
    tokens = picked.reshape(n * capacity, width)
    grads = scaled.reshape(n * capacity, width)

    gate_pre = jnp.dot(tokens, gate_weight[0], preferred_element_type=jnp.float32)
    up_pre = jnp.dot(tokens, up_weight[0], preferred_element_type=jnp.float32)
    hidden_grad = jnp.dot(grads, down_weight[0], preferred_element_type=jnp.float32)
    gate_sig = jax.nn.sigmoid(gate_pre)
    gate_act = gate_pre * gate_sig
    hidden = (gate_act * up_pre).astype(jnp.bfloat16)
    gate_delta = (hidden_grad * up_pre * gate_sig * (1.0 + gate_pre * (1.0 - gate_sig))).astype(
        jnp.bfloat16
    )
    up_delta = (hidden_grad * gate_act).astype(jnp.bfloat16)

    def partial(a, b):
        return lax.dot_general(
            a, b, (((0,), (0,)), ((), ())), preferred_element_type=jnp.float32
        ).astype(jnp.bfloat16)

    pairs = ((grads, hidden), (tokens, gate_delta), (tokens, up_delta))
    if dp == 2:
        half = width // 2
        swap = [(0, 1), (1, 0)]
        leaving = [
            partial(lax.dynamic_slice_in_dim(a, (1 - my_dp) * half, half, 1), b) for a, b in pairs
        ]
        arrived = [lax.ppermute(a, "dp", swap) for a in leaving]
    else:
        leaving = [partial(a, b) for a, b in pairs]
        arrived = [lax.psum_scatter(a, "dp", scatter_dimension=0, tiled=True) for a in leaving]
    key_in, value_in, _ = lax.optimization_barrier((key_rows[0], value_rows[0], leaving))
    k_all, v_all = ring_gather((key_in, value_in), 1)

    out_all = lax.dot_general(
        g_all, out_weight, (((1,), (1,)), ((), ())), preferred_element_type=jnp.float32
    ).astype(jnp.bfloat16)
    out_here = lax.dynamic_slice_in_dim(out_all, me * rows, rows, 0)
    lists = block_lists[0]
    lengths = block_lengths[0]
    block_ids = jnp.arange(blocks, dtype=jnp.int32)
    offsets = jnp.arange(BLK, dtype=jnp.int32)
    valid = offsets[None, :] < lengths[:, None]
    my_list = lax.dynamic_index_in_dim(lists, me, 0, keepdims=False)
    my_blocks = jnp.any(my_list[None, :] == block_ids[:, None], axis=1)
    open_all = (my_blocks[:, None] & valid).astype(jnp.int32).reshape(seq_len, 1)
    offset = jnp.reshape(me * rows, (1,)).astype(jnp.int32)
    query_grad, log_total, row_delta = query_side(
        query_rows[0], k_all, v_all, out_here, open_all, offset
    )
    stats = jnp.stack([log_total[:, 0], row_delta[:, 0]])
    stats_all = lax.all_gather(stats, "ctx", axis=2, tiled=True)
    lists_me = jnp.any(lists == me, axis=1)
    listed = jnp.broadcast_to(lists_me[:, None], (blocks, BLK)).astype(jnp.int32)
    my_open = lax.dynamic_index_in_dim(valid, me, 0, keepdims=False).astype(jnp.int32)
    key_grad, value_grad = key_side(
        key_rows[0],
        value_rows[0],
        q_all,
        out_all,
        stats_all[0][:, None, :],
        stats_all[1][:, None, :],
        listed.reshape(1, seq_len),
        my_open.reshape(BLK, 1),
        offset,
    )
    if dp == 2:
        key_grad, right = lax.optimization_barrier((key_grad, [b for _, b in pairs]))
        sums = [
            partial(lax.dynamic_slice_in_dim(a, my_dp * half, half, 1), b).astype(jnp.float32)
            + r.astype(jnp.float32)
            for (a, _), b, r in zip(pairs, right, arrived)
        ]
    else:
        sums = [r.astype(jnp.float32) for r in arrived]
    down_grad, gate_grad, up_grad = (s[None] for s in sums)
    return (query_grad[None], key_grad[None], value_grad[None], gate_grad, up_grad, down_grad)


def solution(mesh):
    in_specs = (
        P("dp", "ctx", None),
        P("dp", "ctx", None),
        P("dp", "ctx", None),
        P("dp", None, None),
        P("dp", None),
        P(),
        P("dp", "ctx", None),
        P("dp", "ctx", None),
        P("dp", "ctx", None),
        P("dp", "ctx", None),
        P("ctx", None, None),
        P("ctx", None, None),
        P("ctx", None, None),
    )
    out_specs = (
        P("dp", "ctx", None),
        P("dp", "ctx", None),
        P("dp", "ctx", None),
        P("ctx", "dp", None),
        P("ctx", "dp", None),
        P("ctx", "dp", None),
    )
    return jax.shard_map(
        per_device, mesh=mesh, in_specs=in_specs, out_specs=out_specs, check_vma=False
    )
```
